32 devices in a mesh: groups: 2 (over x), wide: 16 (over z, y, core).
Axes of the slice: x: 2, y: 2, z: 4, core: 2. Of those that a mesh axis runs over, the one named last changes fastest.
Arguments:
- fine_field: float32 [256, 64, 512], P(None, ('groups', 'wide')), parts along dimension 1, may hold values from -6 to 6
- w_down_fine: float32 [8, 256, 512], replicated, may hold values from -0.125 to 0.125
- w_conv_mid: float32 [27, 512, 512], P(None, 'wide'), may hold values from -0.0546875 to 0.0546875
- w_down_mid: float32 [8, 512, 1024], P(None, 'wide'), may hold values from -0.09375 to 0.09375
- w_conv_deep: float32 [27, 1024, 1024], P(None, 'wide'), may hold values from -0.0390625 to 0.0390625
- w_up_deep: float32 [8, 1024, 512], P(None, 'wide'), may hold values from -0.1875 to 0.1875
- w_up_mid: float32 [8, 512, 256], replicated, may hold values from -0.25 to 0.25
Outputs:
- fine_update: float32 [256, 64, 512], P(None, ('groups', 'wide')), parts along dimension 1
The draws below stay inside these ranges and needn't reach their ends.
There are 2 independent parts, one for each index of `groups`. The reference program is written for one: setup_inputs(seed, part) draws one part's arguments, and reference() takes and returns one part's arrays. A program takes and returns all parts, laid end to end along the dimension named above; an argument that names none is the same for every part. Nothing has to cross between parts.
All inputs are finite; a program needn't handle non-finite values.
Results may differ from the reference program's by a relative error of at most 0.0001.
Values sent between devices are 32-bit elements; how exact they have to be, the bound alone decides.
A program may use at most 192 MiB of HBM per device.

```python
import jax
import jax.numpy as jnp
from jax import lax

CA = 256
CB = 512
CC = 1024
YA = 32
ZA = 16
NXA = 32


def steps_of(stream_key, dims, split, least, top_value):
    level = 1.0
    for axis_at, parts in split:
        steps = jax.random.uniform(jax.random.fold_in(jax.random.fold_in(stream_key, 6), axis_at), (parts,), jnp.float32, least / len(split), top_value / len(split))
        level = level * jnp.repeat(jnp.exp(steps), dims[axis_at] // parts).reshape((-1,) + (1,) * (len(dims) - 1 - axis_at))
    return level


def bell_draw(own_key, dims, deviation, bound, split=(), dtype=jnp.bfloat16):
    drawn = deviation * jax.random.normal(own_key, dims, jnp.float32)
    if split:
        drawn = drawn * steps_of(own_key, dims, split, -0.22, 0.18)
    return jnp.clip(drawn, -bound, bound).astype(dtype)


def setup_inputs(seed: int = 0, part: int = 0) -> dict:
    arg_keys = jax.random.split(jax.random.key(seed), 8)
    part_keys = jax.random.split(jax.random.fold_in(arg_keys[7], part), 8)
    fine_field = bell_draw(part_keys[0], (CA, NXA, YA * ZA), 1.0, 6.0, ((1, 16),), jnp.float32)
    w_down_fine = bell_draw(arg_keys[1], (8, CA, CB), (8 * CA) ** -0.5, 0.125, (), jnp.float32)
    w_conv_mid = bell_draw(arg_keys[2], (27, CB, CB), (27 * CB) ** -0.5, 0.0546875, ((1, 16),), jnp.float32)
    w_down_mid = bell_draw(arg_keys[3], (8, CB, CC), (8 * CB) ** -0.5, 0.09375, ((1, 16),), jnp.float32)
    w_conv_deep = bell_draw(arg_keys[4], (27, CC, CC), (27 * CC) ** -0.5, 0.0390625, ((1, 16),), jnp.float32)
    w_up_deep = bell_draw(arg_keys[5], (8, CC, CB), CC ** -0.5, 0.1875, ((1, 16),), jnp.float32)
    w_up_mid = bell_draw(arg_keys[6], (8, CB, CA), CB ** -0.5, 0.25, (), jnp.float32)
    return dict(fine_field=fine_field, w_down_fine=w_down_fine, w_conv_mid=w_conv_mid, w_down_mid=w_down_mid, w_conv_deep=w_conv_deep, w_up_deep=w_up_deep, w_up_mid=w_up_mid)


HIGHEST_MODE = lax.Precision.HIGHEST


def convolve_three(field, weights):
    planes, rows, cols = field.shape[1], field.shape[2], field.shape[3]
    padded = jnp.pad(field, ((0, 0), (1, 1), (1, 1), (1, 1)))
    summed = jnp.zeros((weights.shape[1], planes, rows, cols), jnp.float32)
    for a in range(3):
        for b in range(3):
            for c in range(3):
                window = padded[:, a:a + planes, b:b + rows, c:c + cols]
                summed = summed + jnp.einsum("oc,cxyz->oxyz", weights[9 * a + 3 * b + c], window, precision=HIGHEST_MODE)
    return summed


def stride_down(field, weights):
    summed = jnp.zeros((weights.shape[2], field.shape[1] // 2, field.shape[2] // 2, field.shape[3] // 2), jnp.float32)
    for a in range(2):
        for b in range(2):
            for c in range(2):
                window = field[:, a::2, b::2, c::2]
                summed = summed + jnp.einsum("co,cxyz->oxyz", weights[4 * a + 2 * b + c], window, precision=HIGHEST_MODE)
    return summed


def stride_up(field, weights):
    outputs = weights.shape[2]
    planes, rows, cols = field.shape[1], field.shape[2], field.shape[3]
    pieces = [jnp.einsum("co,cxyz->oxyz", weights[tap], field, precision=HIGHEST_MODE) for tap in range(8)]
    stacked = jnp.stack(pieces).reshape(2, 2, 2, outputs, planes, rows, cols)
    return stacked.transpose(3, 4, 0, 5, 1, 6, 2).reshape(outputs, 2 * planes, 2 * rows, 2 * cols)


def reference(fine_field, w_down_fine, w_conv_mid, w_down_mid, w_conv_deep, w_up_deep, w_up_mid):
    fine = fine_field.reshape(CA, NXA, YA, ZA)
    mid_input = stride_down(fine, w_down_fine)
    mid_field = jax.nn.relu(convolve_three(mid_input, w_conv_mid))
    deep_input = jax.nn.relu(stride_down(mid_field, w_down_mid))
    deep_output = jax.nn.relu(convolve_three(deep_input, w_conv_deep))
    mid_merged = jax.nn.relu(mid_field + stride_up(deep_output, w_up_deep))
    fine_update = stride_up(mid_merged, w_up_mid)
    return fine_update.reshape(CA, NXA, YA * ZA)
```

```python
import functools

import jax
import jax.numpy as jnp
from jax import lax
from jax.experimental import pallas as pl
from jax.experimental.pallas import tpu as pltpu
from jax.sharding import PartitionSpec as P

YA = 32
ZA = 16
MESH = pl.DeviceIdType.MESH
BF16 = jnp.bfloat16
F32 = jnp.float32


def selector(rows, cols, copies):
    cells = rows * cols
    small = cells // 4
    source = jnp.arange(copies * cells)[:, None]
    target = jnp.arange(4 * copies * small)[None, :]
    tap = target // (copies * small)
    copy = target // small % copies
    place = target % small
    row = 2 * (place // (cols // 2)) + tap // 2
    col = 2 * (place % (cols // 2)) + tap % 2
    return (source == copy * cells + row * cols + col).astype(F32)


def split(value):
    high = value.astype(BF16)
    return high, (value - high.astype(F32)).astype(BF16)


def dot(left, right):
    return lax.dot_general(left, right, (((1,), (0,)), ((), ())), preferred_element_type=F32)


def dot_nt(left, right):
    return lax.dot_general(left, right, (((1,), (1,)), ((), ())), preferred_element_type=F32)


def dot3(left_high, left_low, right_high, right_low):
    return dot(left_high, right_high) + dot(left_high, right_low) + dot(left_low, right_high)


def middle_kernel(
    wide, groups,
    mid_in, w_mid, w_down, w_deep_hbm, w_up, sel, out,
    xbuf, xh, xl, wmh, wml, acc, mf, wdh, wdl, part, sib, rs, rsin,
    deep_in, wdeep, wch, wcl, deep_out, wup, wuh, wul, mm, landed,
    s1, r1, s2, r2, s3, r3, s_sib, r_sib, s_rs, r_rs, s_up, r_up, s_fw, r_fw, s_aa, r_aa, load_sem,
):
    ny = 2 if wide % 4 == 0 else 1
    nchip = wide // 2
    nz = nchip // ny
    me = lax.axis_index("wide")
    mygroup = lax.axis_index("groups")
    core = me % 2
    chip = me // 2
    y = chip % ny
    z = chip // ny
    mid_local = mf.shape[1]
    cells = mf.shape[2]
    rows, cols = YA // 2, ZA // 2
    drows, dcols = YA // 4, ZA // 4
    dcells = drows * dcols
    deep_local = deep_in.shape[1]
    dn = deep_in.shape[2]
    ngr = dn // cells

    load = pltpu.make_async_copy(w_deep_hbm, wdeep, load_sem)
    load.start()

    barrier = pltpu.get_barrier_semaphore()
    for step in range(1, wide):
        pl.semaphore_signal(barrier, inc=1, device_id={"wide": (me + step) % wide}, device_id_type=MESH)
    for step in range(1, groups):
        pl.semaphore_signal(barrier, inc=1, device_id={"groups": (mygroup + step) % groups}, device_id_type=MESH)
    pl.semaphore_wait(barrier, wide + groups - 2)

    def slot(zz, yy, cc):
        return (zz * ny + yy) * 2 + cc

    def gather(buf, send_sem, recv_sem, consume, idle):
        def move(at, target, k):
            return pltpu.make_async_remote_copy(
                src_ref=buf.at[at], dst_ref=buf.at[at], send_sem=send_sem.at[k], recv_sem=recv_sem.at[at],
                device_id={"wide": target}, device_id_type=MESH)

        def arrived(at):
            move(at, slot(z, y, 1 - core), 0).wait_recv()

        sibling = slot(z, y, 1 - core)
        other = slot(z, ny - 1 - y, core)
        if ny == 2:
            move(me, other, nz).start()
        move(me, sibling, 2 * nz).start()
        for dz in range(1, nz):
            move(me, slot((z + nz - dz) % nz, y, core), dz - 1).start()
        idle()
        arrived(sibling)
        consume(chip)

        def other_row(dz):
            zp = (z + dz) % nz
            at = slot(zp, 1 - y, core)
            arrived(at)
            move(at, sibling, 2 * nz + dz * ny + 1).start()

        def step(dz, carry):
            zs = (z + dz) % nz
            at = slot(zs, y, core)
            arrived(at)
            if ny == 2:
                move(at, other, nz + dz).start()
            move(at, sibling, 2 * nz + dz * ny).start()
            if ny == 2:
                other_row(dz - 1)
            arrived(slot(zs, y, 1 - core))
            consume(zs * ny + y)
            if ny == 2:
                zp = (z + dz - 1) % nz
                arrived(slot(zp, 1 - y, 1 - core))
                consume(zp * ny + 1 - y)
            return carry

        lax.fori_loop(1, nz, step, 0)
        if ny == 2:
            other_row(nz - 1)
            zp = (z + nz - 1) % nz
            arrived(slot(zp, 1 - y, 1 - core))
            consume(zp * ny + 1 - y)

        def finish():
            for k in range(nz - 1):
                move(me, sibling, k).wait_send()
            if ny == 2:
                for k in range(nz):
                    move(me, sibling, nz + k).wait_send()
            for k in range(nz * ny):
                move(me, sibling, 2 * nz + k).wait_send()

        return finish

    xbuf[me] = mid_in[...]
    taps = 9 * mid_local
    lane = lax.broadcasted_iota(jnp.int32, (mid_local, cells), 1)
    mid_masks = {}
    for b in range(3):
        for c in range(3):
            r, s = lane // cols + b - 1, lane % cols + c - 1
            mid_masks[b, c] = (r >= 0) & (r < rows) & (s >= 0) & (s < cols)

    def convolve_mid(at):
        for h in range(2):
            high, low = split(xbuf[at * 2 + h])
            xh[:, h * cells:(h + 1) * cells] = high
            xl[:, h * cells:(h + 1) * cells] = low

        def plane_tap(a, carry):
            here = pl.ds(pl.multiple_of(a * taps, taps), taps)
            product = dot3(wmh[here, :], wml[here, :], xh[...], xl[...])
            for h in range(2):
                total = jnp.zeros((mid_local, cells), F32)
                for b in range(3):
                    for c in range(3):
                        tap = 3 * b + c
                        piece = product[tap * mid_local:(tap + 1) * mid_local, h * cells:(h + 1) * cells]
                        offset = (b - 1) * cols + c - 1
                        if offset:
                            piece = pltpu.roll(piece, (-offset) % cells, 1)
                            piece = jnp.where(mid_masks[b, c], piece, 0.0)
                        total = total + piece
                acc[at * 2 + h - a + 2] += total
            return carry

        lax.fori_loop(0, 3, plane_tap, 0)

    def prepare_mid():
        acc[...] = jnp.zeros_like(acc)
        wmh[...], wml[...] = split(w_mid[...])
        wdh[...], wdl[...] = split(w_down[...].T)

    finish_mid = gather(xbuf, s1, r1, convolve_mid, prepare_mid)

    share = wup.shape[1] // groups
    mine = pl.ds(pl.multiple_of(mygroup * share, share), share)

    def up_move(target, source):
        return pltpu.make_async_remote_copy(
            src_ref=w_up.at[target, mine], dst_ref=wup.at[me, mine], send_sem=s_up.at[target], recv_sem=r_up.at[source],
            device_id={"wide": target}, device_id_type=MESH)

    def up_arrived(source):
        pltpu.make_async_remote_copy(
            src_ref=w_up.at[source, mine], dst_ref=wup.at[source, mine], send_sem=s_up.at[source], recv_sem=r_up.at[source],
            device_id={"wide": source}, device_id_type=MESH).wait_recv()

    mf[...] = jnp.maximum(acc[1:wide + 1], 0.0)

    gathered = []
    for a in range(2):
        for g in range(ngr):
            gathered.append(jnp.concatenate([mf[2 * (4 * g + p) + a] for p in range(4)], axis=1))
    high, low = split(jnp.concatenate(gathered, axis=0))
    high, low = dot(high, sel[...]).astype(BF16), dot(low, sel[...]).astype(BF16)

    def spread_rows(value):
        blocks = []
        for a in range(2):
            for bc in range(4):
                blocks.append(jnp.concatenate([
                    value[(a * ngr + g) * mid_local:(a * ngr + g + 1) * mid_local, bc * cells:(bc + 1) * cells]
                    for g in range(ngr)], axis=1))
        return jnp.concatenate(blocks, axis=0)

    high, low = spread_rows(high), spread_rows(low)
    part[...] = dot3(wdh[...], wdl[...], high, low).reshape(part.shape)
    sibling_id = chip * 2 + 1 - core
    pair = pltpu.make_async_remote_copy(
        src_ref=part.at[:, 1 - core], dst_ref=sib, send_sem=s_sib, recv_sem=r_sib,
        device_id={"wide": sibling_id}, device_id_type=MESH)
    pair.start()

    load.wait()

    def split_deep(t, carry):
        here = pl.ds(pl.multiple_of(t * deep_local, deep_local), deep_local)
        wch[here, :], wcl[here, :] = split(wdeep[here, :])
        return carry

    pair.wait_recv()

    def rs_move(target, source, k):
        return pltpu.make_async_remote_copy(
            src_ref=rs.at[target], dst_ref=rsin.at[source], send_sem=s_rs.at[k], recv_sem=r_rs.at[source],
            device_id={"wide": target * 2 + core}, device_id_type=MESH)

    for step in range(1, nchip):
        target = (chip + step) % nchip
        rs[target] = part[target, core] + sib[target]
        rs_move(target, chip, step).start()
    for step in range(1, wide):
        target = (me + step) % wide
        up_move(target, me).start()
    wup[me, mine] = w_up[me, mine]
    lax.fori_loop(0, 27, split_deep, 0)
    total = part[chip, core] + sib[chip]
    for step in range(1, nchip):
        source = (chip + nchip - step) % nchip
        rs_move(source, source, step).wait_recv()
        total = total + rsin[source]
    deep_in[me] = jnp.maximum(total, 0.0)

    def nothing(*args):
        return None

    finish_in = gather(deep_in, s2, r2, nothing, nothing)
    for step in range(1, wide):
        up_arrived((me + wide - step) % wide)

    def forward(target, source):
        return pltpu.make_async_remote_copy(
            src_ref=wup.at[:, mine], dst_ref=wup.at[:, mine], send_sem=s_fw.at[target], recv_sem=r_fw.at[mygroup],
            device_id={"groups": target}, device_id_type=MESH)

    for step in range(1, groups):
        forward((mygroup + step) % groups, mygroup).start()

    dh, dl = split(deep_in[...].reshape(wide * deep_local, dn))
    dlane = lax.broadcasted_iota(jnp.int32, (deep_local, dn), 1)
    total = jnp.zeros((deep_local, dn), F32)
    for a in range(3):
        here = slice(a * 9 * deep_local, (a + 1) * 9 * deep_local)
        product = dot3(wch[here, :], wcl[here, :], dh, dl)
        for b in range(3):
            for c in range(3):
                tap = 3 * b + c
                piece = product[tap * deep_local:(tap + 1) * deep_local]
                offset = (a - 1) * dcells + (b - 1) * dcols + c - 1
                if offset:
                    piece = pltpu.roll(piece, (-offset) % dn, 1)
                    p, r, s = dlane // dcells + a - 1, dlane // dcols % drows + b - 1, dlane % dcols + c - 1
                    inside = (p >= 0) & (p < dn // dcells) & (r >= 0) & (r < drows) & (s >= 0) & (s < dcols)
                    piece = jnp.where(inside, piece, 0.0)
                total = total + piece
    deep_out[me] = jnp.maximum(total, 0.0)

    def prepare_up():
        for step in range(1, groups):
            source = (mygroup + groups - step) % groups
            theirs = pl.ds(pl.multiple_of(source * share, share), share)
            pltpu.make_async_remote_copy(
                src_ref=wup.at[:, theirs], dst_ref=wup.at[:, theirs], send_sem=s_fw.at[source],
                recv_sem=r_fw.at[source], device_id={"groups": source}, device_id_type=MESH).wait_recv()
        wuh[...], wul[...] = split(wup[...].reshape(wide * deep_local, wup.shape[2]).T)

    finish_out = gather(deep_out, s3, r3, nothing, prepare_up)
    dh, dl = split(deep_out[...].reshape(wide * deep_local, dn))
    lifted = dot3(wuh[...], wul[...], dh, dl)
    blocks = []
    for a in range(2):
        for g in range(ngr):
            blocks.append(jnp.concatenate([
                lifted[(a * 4 + bc) * mid_local:(a * 4 + bc + 1) * mid_local, g * cells:(g + 1) * cells]
                for bc in range(4)], axis=1))
    high, low = split(jnp.concatenate(blocks, axis=0))
    spread = dot_nt(high, sel[...]) + dot_nt(low, sel[...])
    for a in range(2):
        for g in range(ngr):
            for p in range(4):
                plane = 2 * (4 * g + p) + a
                block = spread[(a * ngr + g) * mid_local:(a * ngr + g + 1) * mid_local, p * cells:(p + 1) * cells]
                mm[plane] = jnp.maximum(mf[plane] + block, 0.0)

    def plane_move(target, source):
        return pltpu.make_async_remote_copy(
            src_ref=mm.at[target], dst_ref=landed.at[source], send_sem=s_aa.at[target], recv_sem=r_aa.at[source],
            device_id={"wide": target}, device_id_type=MESH)

    for step in range(1, wide):
        plane_move((me + step) % wide, me).start()
    landed[me] = mm[me]
    finish_mid()
    finish_in()
    finish_out()
    pair.wait_send()
    for step in range(1, nchip):
        rs_move((chip + step) % nchip, chip, step).wait_send()
    for step in range(1, wide):
        up_move((me + step) % wide, me).wait_send()
    for step in range(1, groups):
        forward((mygroup + step) % groups, mygroup).wait_send()
    for step in range(1, wide):
        plane_move((me + step) % wide, me).wait_send()
    for step in range(1, wide):
        source = (me + wide - step) % wide
        plane_move(source, source).wait_recv()
    out[...] = landed[...]


def shards(wide, groups, fine_field, w_down_fine, w_conv_mid, w_down_mid, w_conv_deep, w_up_deep, w_up_mid):
    chan_fine = fine_field.shape[0]
    chan_mid = w_down_fine.shape[2]
    chan_deep = w_down_mid.shape[2]
    mid_local = w_conv_mid.shape[1]
    deep_local = w_conv_deep.shape[1]
    cells = YA // 2 * (ZA // 2)
    dn = wide // 2 * (cells // 4)
    nchip = wide // 2
    high = lax.Precision.HIGH

    fine_sel = selector(YA, ZA, 1)
    picks = jnp.dot(fine_field.reshape(chan_fine * 2, YA * ZA), fine_sel, precision=high)
    picks = picks.reshape(chan_fine, 2, 4, cells).transpose(1, 2, 0, 3).reshape(8 * chan_fine, cells)
    mid_input = lax.dot_general(
        w_down_fine.reshape(8 * chan_fine, chan_mid), picks, (((0,), (0,)), ((), ())), precision=high)
    up_blocks = w_up_deep.reshape(8, deep_local, wide, mid_local).transpose(2, 1, 0, 3)
    up_blocks = up_blocks.reshape(wide, deep_local, 8 * mid_local)
    sel = selector(YA // 2, ZA // 2, 4).astype(BF16)

    vmem = pl.BlockSpec(memory_space=pltpu.VMEM)
    dma = pltpu.SemaphoreType.DMA
    sends = 4 * nchip
    merged = pl.pallas_call(
        functools.partial(middle_kernel, wide, groups),
        out_shape=jax.ShapeDtypeStruct((wide, mid_local, cells), F32),
        in_specs=[vmem, vmem, vmem, pl.BlockSpec(memory_space=pl.ANY), vmem, vmem],
        out_specs=vmem,
        scratch_shapes=[
            pltpu.VMEM((wide, chan_mid, cells), F32),
            pltpu.VMEM((chan_mid, 2 * cells), BF16),
            pltpu.VMEM((chan_mid, 2 * cells), BF16),
            pltpu.VMEM((27 * mid_local, chan_mid), BF16),
            pltpu.VMEM((27 * mid_local, chan_mid), BF16),
            pltpu.VMEM((wide + 2, mid_local, cells), F32),
            pltpu.VMEM((wide, mid_local, cells), F32),
            pltpu.VMEM((chan_deep, 8 * mid_local), BF16),
            pltpu.VMEM((chan_deep, 8 * mid_local), BF16),
            pltpu.VMEM((nchip, 2, deep_local, dn), F32),
            pltpu.VMEM((nchip, deep_local, dn), F32),
            pltpu.VMEM((nchip, deep_local, dn), F32),
            pltpu.VMEM((nchip, deep_local, dn), F32),
            pltpu.VMEM((wide, deep_local, dn), F32),
            pltpu.VMEM((27 * deep_local, chan_deep), F32),
            pltpu.VMEM((27 * deep_local, chan_deep), BF16),
            pltpu.VMEM((27 * deep_local, chan_deep), BF16),
            pltpu.VMEM((wide, deep_local, dn), F32),
            pltpu.VMEM((wide, deep_local, 8 * mid_local), F32),
            pltpu.VMEM((8 * mid_local, chan_deep), BF16),
            pltpu.VMEM((8 * mid_local, chan_deep), BF16),
            pltpu.VMEM((wide, mid_local, cells), F32),
            pltpu.VMEM((wide, mid_local, cells), F32),
            dma((sends,)), dma((wide,)),
            dma((sends,)), dma((wide,)),
            dma((sends,)), dma((wide,)),
            dma, dma,
            dma((nchip,)), dma((nchip,)),
            dma((wide,)), dma((wide,)),
            dma((groups,)), dma((groups,)),
            dma((wide,)), dma((wide,)),
            dma,
        ],
        compiler_params=pltpu.CompilerParams(
            collective_id=0, has_side_effects=True, vmem_limit_bytes=56 * 1024 * 1024),
    )(
        mid_input,
        w_conv_mid.reshape(27 * mid_local, chan_mid),
        w_down_mid.reshape(8 * mid_local, chan_deep),
        w_conv_deep.reshape(27 * deep_local, chan_deep),
        up_blocks,
        sel,
    )
    merged = merged.reshape(chan_mid, cells)
    lifted = lax.dot_general(
        w_up_mid, merged, (((1,), (0,)), ((), ())), precision=high)
    lifted = lifted.reshape(2, 4, chan_fine, cells).transpose(2, 0, 1, 3).reshape(chan_fine * 2, 4 * cells)
    return jnp.dot(lifted, fine_sel.T, precision=high).reshape(chan_fine, 2, YA * ZA)


def solution(mesh):
    wide, groups = mesh.shape["wide"], mesh.shape["groups"]
    return jax.shard_map(
        functools.partial(shards, wide, groups),
        mesh=mesh,
        in_specs=(
            P(None, ("groups", "wide"), None),
            P(),
            P(None, "wide", None),
            P(None, "wide", None),
            P(None, "wide", None),
            P(None, "wide", None),
            P(),
        ),
        out_specs=P(None, ("groups", "wide"), None),
        check_vma=False,
    )
```

```python
import functools

import jax
import jax.numpy as jnp
import numpy as np
from jax import lax
from jax.experimental import pallas as pl
from jax.experimental.pallas import tpu as pltpu
from jax.sharding import PartitionSpec as P

YA = 32
ZA = 16
MESH = pl.DeviceIdType.MESH
BF16 = jnp.bfloat16
F32 = jnp.float32


def selector(rows, cols, copies):
    cells = rows * cols
    small = cells // 4
    source = np.arange(copies * cells)[:, None]
    target = np.arange(4 * copies * small)[None, :]
    tap = target // (copies * small)
    copy = target // small % copies
    place = target % small
    row = 2 * (place // (cols // 2)) + tap // 2
    col = 2 * (place % (cols // 2)) + tap % 2
    return (source == copy * cells + row * cols + col).astype(np.float32)


def split(value):
    high = value.astype(BF16)
    return high, (value - high.astype(F32)).astype(BF16)


def dot(left, right):
    return lax.dot_general(left, right, (((1,), (0,)), ((), ())), preferred_element_type=F32)


def dot_nt(left, right):
    return lax.dot_general(left, right, (((1,), (1,)), ((), ())), preferred_element_type=F32)


def dot3(left_high, left_low, right_high, right_low):
    return dot(left_high, right_high) + dot(left_high, right_low) + dot(left_low, right_high)


def middle_kernel(
    wide, groups,
    fine, w_fine_hbm, w_mid_hbm, w_down_hbm, w_deep_hbm, w_up_hbm, w_last_hbm, sel, fsel, out,
    w_fine, w_mid, w_down, w_up_all, w_last, w_up, wfh, wfl, wlh, wll, pacc, xbuf, xh, xl, wmh, wml, acc, mf, wdh, wdl, part, sib, rs, rsin,
    deep_in, wdeep, wch, wcl, deep_out, wup, wuh, wul, mm, landed,
    s1, r1, s2, r2, s3, r3, s_sib, r_sib, s_rs, r_rs, s_up, r_up, s_fw, r_fw, s_aa, r_aa, load_sems,
):
    ny = 2 if wide % 4 == 0 else 1
    nchip = wide // 2
    nz = nchip // ny
    me = lax.axis_index("wide")
    mygroup = lax.axis_index("groups")
    core = me % 2
    chip = me // 2
    y = chip % ny
    z = chip // ny
    mid_local = mf.shape[1]
    chan_mid = xbuf.shape[1]
    cells = mf.shape[2]
    rows, cols = YA // 2, ZA // 2
    drows, dcols = YA // 4, ZA // 4
    dcells = drows * dcols
    deep_local = deep_in.shape[1]
    dn = deep_in.shape[2]
    ngr = dn // cells

    third = wdeep.shape[1]

    def deep_load(k):
        return pltpu.make_async_copy(w_deep_hbm.at[pl.ds(k * third, third)], wdeep.at[k % 2], load_sems.at[5 + k])

    sources = (w_up_hbm, w_fine_hbm, w_mid_hbm, w_down_hbm, w_last_hbm)
    places = (w_up_all, w_fine, w_mid, w_down, w_last)
    loads = [pltpu.make_async_copy(a, b, load_sems.at[k]) for k, (a, b) in enumerate(zip(sources, places))]
    load_up, load_fine, load_mid, load_down, load_last = loads
    for load in loads + [deep_load(0), deep_load(1)]:
        load.start()

    barrier = pltpu.get_barrier_semaphore()
    for step in range(1, wide):
        pl.semaphore_signal(barrier, inc=1, device_id={"wide": (me + step) % wide}, device_id_type=MESH)
    for step in range(1, groups):
        pl.semaphore_signal(barrier, inc=1, device_id={"groups": (mygroup + step) % groups}, device_id_type=MESH)
    pl.semaphore_wait(barrier, wide + groups - 2)

    def slot(zz, yy, cc):
        return (zz * ny + yy) * 2 + cc

    def gather(buf, send_sem, recv_sem, consume, idle):
        def move(at, target, k):
            return pltpu.make_async_remote_copy(
                src_ref=buf.at[at], dst_ref=buf.at[at], send_sem=send_sem.at[k], recv_sem=recv_sem.at[at],
                device_id={"wide": target}, device_id_type=MESH)

        def arrived(at):
            move(at, slot(z, y, 1 - core), 0).wait_recv()

        sibling = slot(z, y, 1 - core)
        other = slot(z, ny - 1 - y, core)
        if ny == 2:
            move(me, other, nz).start()
        move(me, sibling, 2 * nz).start()
        for dz in range(1, nz):
            move(me, slot((z + nz - dz) % nz, y, core), dz - 1).start()
        idle()
        arrived(sibling)
        consume(chip)

        def other_row(dz):
            zp = (z + dz) % nz
            at = slot(zp, 1 - y, core)
            arrived(at)
            move(at, sibling, 2 * nz + dz * ny + 1).start()

        def step(dz, carry):
            zs = (z + dz) % nz
            at = slot(zs, y, core)
            arrived(at)
            if ny == 2:
                move(at, other, nz + dz).start()
            move(at, sibling, 2 * nz + dz * ny).start()
            if ny == 2:
                other_row(dz - 1)
            arrived(slot(zs, y, 1 - core))
            consume(zs * ny + y)
            if ny == 2:
                zp = (z + dz - 1) % nz
                arrived(slot(zp, 1 - y, 1 - core))
                consume(zp * ny + 1 - y)
            return carry

        lax.fori_loop(1, nz, step, 0)
        if ny == 2:
            other_row(nz - 1)
            zp = (z + nz - 1) % nz
            arrived(slot(zp, 1 - y, 1 - core))
            consume(zp * ny + 1 - y)

        def finish():
            for k in range(nz - 1):
                move(me, sibling, k).wait_send()
            if ny == 2:
                for k in range(nz):
                    move(me, sibling, nz + k).wait_send()
            for k in range(nz * ny):
                move(me, sibling, 2 * nz + k).wait_send()

        return finish

    share = wup.shape[1] // groups
    mine = pl.ds(pl.multiple_of(mygroup * share, share), share)

    def up_move(target, source):
        return pltpu.make_async_remote_copy(
            src_ref=w_up.at[target], dst_ref=wup.at[me, mine], send_sem=s_up.at[target], recv_sem=r_up.at[source],
            device_id={"wide": target}, device_id_type=MESH)

    def up_arrived(source):
        pltpu.make_async_remote_copy(
            src_ref=w_up.at[source], dst_ref=wup.at[source, mine], send_sem=s_up.at[source], recv_sem=r_up.at[source],
            device_id={"wide": source}, device_id_type=MESH).wait_recv()

    load_up.wait()
    pieces = [w_up_all[t, mine, :] for t in range(8)]
    for d in range(wide):
        w_up[d] = jnp.concatenate([piece[:, d * mid_local:(d + 1) * mid_local] for piece in pieces], axis=1)
    for step in range(1, wide):
        up_move((me + step) % wide, me).start()
    wup[me, mine] = w_up[me]

    chan_fine = fine.shape[0]
    picked_high, picked_low = [], []
    for a in range(2):
        high, low = split(fine[:, a, :])
        high, low = dot_nt(fsel[...], high).astype(BF16), dot_nt(fsel[...], low).astype(BF16)
        for bc in range(4):
            picked_high.append(high[bc * cells:(bc + 1) * cells])
            picked_low.append(low[bc * cells:(bc + 1) * cells])
    picked_high = jnp.concatenate(picked_high, axis=1)
    picked_low = jnp.concatenate(picked_low, axis=1)
    load_fine.wait()

    def split_fine(t, carry):
        here = pl.ds(pl.multiple_of(t * chan_fine, chan_fine), chan_fine)
        wfh[here, :], wfl[here, :] = split(w_fine[here, :])
        return carry

    lax.fori_loop(0, 8, split_fine, 0)
    both = dot(jnp.concatenate([picked_high, picked_low], axis=0), wfh[...])
    xbuf[me] = (both[:cells] + both[cells:] + dot(picked_high, wfl[...])).T
    taps = 9 * mid_local
    lane = lax.broadcasted_iota(jnp.int32, (mid_local, cells), 1)
    mid_masks = {}
    for b in range(3):
        for c in range(3):
            r, s = lane // cols + b - 1, lane % cols + c - 1
            mid_masks[b, c] = (r >= 0) & (r < rows) & (s >= 0) & (s < cols)

    def convolve_mid(at):
        for h in range(2):
            high, low = split(xbuf[at * 2 + h])
            xh[:, h * cells:(h + 1) * cells] = high
            xl[:, h * cells:(h + 1) * cells] = low

        def plane_tap(a, carry):
            here = pl.ds(pl.multiple_of(a * taps, taps), taps)
            product = dot3(wmh[here, :], wml[here, :], xh[...], xl[...])
            for h in range(2):
                total = jnp.zeros((mid_local, cells), F32)
                for b in range(3):
                    for c in range(3):
                        tap = 3 * b + c
                        piece = product[tap * mid_local:(tap + 1) * mid_local, h * cells:(h + 1) * cells]
                        offset = (b - 1) * cols + c - 1
                        if offset:
                            piece = pltpu.roll(piece, (-offset) % cells, 1)
                            piece = jnp.where(mid_masks[b, c], piece, 0.0)
                        total = total + piece
                acc[at * 2 + h - a + 2] += total
            return carry

        lax.fori_loop(0, 3, plane_tap, 0)

    def prepare_mid():
        acc[...] = jnp.zeros_like(acc)
        load_mid.wait()
        load_down.wait()
        wmh[...], wml[...] = split(w_mid[...])
        wdh[...], wdl[...] = split(w_down[...].T)

    finish_mid = gather(xbuf, s1, r1, convolve_mid, prepare_mid)

    mf[...] = jnp.maximum(acc[1:wide + 1], 0.0)

    gathered = []
    for a in range(2):
        for g in range(ngr):
            gathered.append(jnp.concatenate([mf[2 * (4 * g + p) + a] for p in range(4)], axis=1))
    high, low = split(jnp.concatenate(gathered, axis=0))
    high, low = dot(high, sel[...]).astype(BF16), dot(low, sel[...]).astype(BF16)

    def spread_rows(value):
        blocks = []
        for a in range(2):
            for bc in range(4):
                blocks.append(jnp.concatenate([
                    value[(a * ngr + g) * mid_local:(a * ngr + g + 1) * mid_local, bc * cells:(bc + 1) * cells]
                    for g in range(ngr)], axis=1))
        return jnp.concatenate(blocks, axis=0)

    high, low = spread_rows(high), spread_rows(low)
    part[...] = dot3(wdh[...], wdl[...], high, low).reshape(part.shape)
    sibling_id = chip * 2 + 1 - core
    pair = pltpu.make_async_remote_copy(
        src_ref=part.at[:, 1 - core], dst_ref=sib, send_sem=s_sib, recv_sem=r_sib,
        device_id={"wide": sibling_id}, device_id_type=MESH)
    pair.start()

    def split_deep(k):
        def block(t, carry):
            here = pl.ds(pl.multiple_of(t * deep_local, deep_local), deep_local)
            there = pl.ds(pl.multiple_of(k * third + t * deep_local, deep_local), deep_local)
            wch[there, :], wcl[there, :] = split(wdeep[k % 2, here, :])
            return carry

        lax.fori_loop(0, 9, block, 0)

    pair.wait_recv()

    def rs_move(target, source, k):
        return pltpu.make_async_remote_copy(
            src_ref=rs.at[target], dst_ref=rsin.at[source], send_sem=s_rs.at[k], recv_sem=r_rs.at[source],
            device_id={"wide": target * 2 + core}, device_id_type=MESH)

    for step in range(1, nchip):
        target = (chip + step) % nchip
        rs[target] = part[target, core] + sib[target]
        rs_move(target, chip, step).start()
    deep_load(0).wait()
    split_deep(0)
    deep_load(2).start()
    deep_load(1).wait()
    split_deep(1)
    deep_load(2).wait()
    split_deep(2)
    total = part[chip, core] + sib[chip]
    for step in range(1, nchip):
        source = (chip + nchip - step) % nchip
        rs_move(source, source, step).wait_recv()
        total = total + rsin[source]
    deep_in[me] = jnp.maximum(total, 0.0)

    def nothing(*args):
        return None

    def forward(target, source):
        return pltpu.make_async_remote_copy(
            src_ref=wup.at[:, mine], dst_ref=wup.at[:, mine], send_sem=s_fw.at[target], recv_sem=r_fw.at[mygroup],
            device_id={"groups": target}, device_id_type=MESH)

    def prepare_deep():
        for step in range(1, wide):
            up_arrived((me + wide - step) % wide)
        for step in range(1, groups):
            forward((mygroup + step) % groups, mygroup).start()
        load_last.wait()
        for t in range(8):
            here = pl.ds(t * chan_mid, chan_mid)
            wlh[here, :], wll[here, :] = split(w_last[here, :])

    chip_rows = 2 * deep_local
    by_chip = chip_rows % 128 == 0

    def convolve_deep(at):
        high, low = split(deep_in[pl.ds(at * 2, 2)].reshape(chip_rows, dn))
        lanes = pl.ds(pl.multiple_of(at * chip_rows, chip_rows), chip_rows)

        def plane_tap(a, carry):
            here = pl.ds(pl.multiple_of(a * 9 * deep_local, 9 * deep_local), 9 * deep_local)
            pacc[here, :] += dot3(wch[here, lanes], wcl[here, lanes], high, low)
            return carry

        lax.fori_loop(0, 3, plane_tap, 0)

    if by_chip:
        pacc[...] = jnp.zeros_like(pacc)
        finish_in = gather(deep_in, s2, r2, convolve_deep, prepare_deep)
    else:
        finish_in = gather(deep_in, s2, r2, nothing, prepare_deep)
        dh, dl = split(deep_in[...].reshape(wide * deep_local, dn))
        pacc[...] = dot3(wch[...], wcl[...], dh, dl)
    dlane = lax.broadcasted_iota(jnp.int32, (deep_local, dn), 1)
    total = jnp.zeros((deep_local, dn), F32)
    for a in range(3):
        for b in range(3):
            for c in range(3):
                tap = 3 * b + c
                at = (9 * a + tap) * deep_local
                piece = pacc[at:at + deep_local, :]
                offset = (a - 1) * dcells + (b - 1) * dcols + c - 1
                if offset:
                    piece = pltpu.roll(piece, (-offset) % dn, 1)
                    p, r, s = dlane // dcells + a - 1, dlane // dcols % drows + b - 1, dlane % dcols + c - 1
                    inside = (p >= 0) & (p < dn // dcells) & (r >= 0) & (r < drows) & (s >= 0) & (s < dcols)
                    piece = jnp.where(inside, piece, 0.0)
                total = total + piece
    deep_out[me] = jnp.maximum(total, 0.0)

    def prepare_up():
        for step in range(1, groups):
            source = (mygroup + groups - step) % groups
            theirs = pl.ds(pl.multiple_of(source * share, share), share)
            pltpu.make_async_remote_copy(
                src_ref=wup.at[:, theirs], dst_ref=wup.at[:, theirs], send_sem=s_fw.at[source],
                recv_sem=r_fw.at[source], device_id={"groups": source}, device_id_type=MESH).wait_recv()
        wuh[...], wul[...] = split(wup[...].reshape(wide * deep_local, wup.shape[2]).T)

    finish_out = gather(deep_out, s3, r3, nothing, prepare_up)
    dh, dl = split(deep_out[...].reshape(wide * deep_local, dn))
    lifted = dot3(wuh[...], wul[...], dh, dl)
    blocks = []
    for a in range(2):
        for g in range(ngr):
            blocks.append(jnp.concatenate([
                lifted[(a * 4 + bc) * mid_local:(a * 4 + bc + 1) * mid_local, g * cells:(g + 1) * cells]
                for bc in range(4)], axis=1))
    high, low = split(jnp.concatenate(blocks, axis=0))
    spread = dot_nt(high, sel[...]) + dot_nt(low, sel[...])
    for a in range(2):
        for g in range(ngr):
            for p in range(4):
                plane = 2 * (4 * g + p) + a
                block = spread[(a * ngr + g) * mid_local:(a * ngr + g + 1) * mid_local, p * cells:(p + 1) * cells]
                mm[plane] = jnp.maximum(mf[plane] + block, 0.0)

    def plane_move(target, source):
        return pltpu.make_async_remote_copy(
            src_ref=mm.at[target], dst_ref=landed.at[source], send_sem=s_aa.at[target], recv_sem=r_aa.at[source],
            device_id={"wide": target}, device_id_type=MESH)

    for step in range(1, wide):
        plane_move((me + step) % wide, me).start()
    landed[me] = mm[me]
    finish_mid()
    finish_in()
    finish_out()
    pair.wait_send()
    for step in range(1, nchip):
        rs_move((chip + step) % nchip, chip, step).wait_send()
    for step in range(1, wide):
        up_move((me + step) % wide, me).wait_send()
    for step in range(1, groups):
        forward((mygroup + step) % groups, mygroup).wait_send()
    for step in range(1, wide):
        plane_move((me + step) % wide, me).wait_send()
    for step in range(1, wide):
        source = (me + wide - step) % wide
        plane_move(source, source).wait_recv()

    high, low = split(landed[...].reshape(chan_mid, cells).T)
    both = jnp.concatenate([high, low], axis=0)
    for a in range(2):
        rows_of = []
        for bc in range(4):
            here = pl.ds((4 * a + bc) * chan_mid, chan_mid)
            twice = dot(both, wlh[here, :])
            rows_of.append(twice[:cells] + twice[cells:] + dot(high, wll[here, :]))
        last_high, last_low = split(jnp.concatenate(rows_of, axis=0).T)
        out[:, a, :] = dot(last_high, fsel[...]) + dot(last_low, fsel[...])


def shards(wide, groups, fine_field, w_down_fine, w_conv_mid, w_down_mid, w_conv_deep, w_up_deep, w_up_mid):
    chan_fine = fine_field.shape[0]
    chan_mid = w_down_fine.shape[2]
    chan_deep = w_down_mid.shape[2]
    mid_local = w_conv_mid.shape[1]
    deep_local = w_conv_deep.shape[1]
    cells = YA // 2 * (ZA // 2)
    dn = wide // 2 * (cells // 4)
    nchip = wide // 2
    fine_sel = jnp.asarray(selector(YA, ZA, 1).T, dtype=BF16)
    sel = jnp.asarray(selector(YA // 2, ZA // 2, 4), dtype=BF16)

    vmem = pl.BlockSpec(memory_space=pltpu.VMEM)
    dma = pltpu.SemaphoreType.DMA
    sends = 4 * nchip
    anywhere = pl.BlockSpec(memory_space=pl.ANY)
    return pl.pallas_call(
        functools.partial(middle_kernel, wide, groups),
        out_shape=jax.ShapeDtypeStruct(fine_field.shape, F32),
        in_specs=[vmem] + [anywhere] * 6 + [vmem, vmem],
        out_specs=vmem,
        scratch_shapes=[
            pltpu.VMEM((8 * chan_fine, chan_mid), F32),
            pltpu.VMEM((27 * mid_local, chan_mid), F32),
            pltpu.VMEM((8 * mid_local, chan_deep), F32),
            pltpu.VMEM((8, deep_local, chan_mid), F32),
            pltpu.VMEM((8 * chan_mid, chan_fine), F32),
            pltpu.VMEM((wide, deep_local // groups, 8 * mid_local), F32),
            pltpu.VMEM((8 * chan_fine, chan_mid), BF16),
            pltpu.VMEM((8 * chan_fine, chan_mid), BF16),
            pltpu.VMEM((8 * chan_mid, chan_fine), BF16),
            pltpu.VMEM((8 * chan_mid, chan_fine), BF16),
            pltpu.VMEM((27 * deep_local, dn), F32),
            pltpu.VMEM((wide, chan_mid, cells), F32),
            pltpu.VMEM((chan_mid, 2 * cells), BF16),
            pltpu.VMEM((chan_mid, 2 * cells), BF16),
            pltpu.VMEM((27 * mid_local, chan_mid), BF16),
            pltpu.VMEM((27 * mid_local, chan_mid), BF16),
            pltpu.VMEM((wide + 2, mid_local, cells), F32),
            pltpu.VMEM((wide, mid_local, cells), F32),
            pltpu.VMEM((chan_deep, 8 * mid_local), BF16),
            pltpu.VMEM((chan_deep, 8 * mid_local), BF16),
            pltpu.VMEM((nchip, 2, deep_local, dn), F32),
            pltpu.VMEM((nchip, deep_local, dn), F32),
            pltpu.VMEM((nchip, deep_local, dn), F32),
            pltpu.VMEM((nchip, deep_local, dn), F32),
            pltpu.VMEM((wide, deep_local, dn), F32),
            pltpu.VMEM((2, 9 * deep_local, chan_deep), F32),
            pltpu.VMEM((27 * deep_local, chan_deep), BF16),
            pltpu.VMEM((27 * deep_local, chan_deep), BF16),
            pltpu.VMEM((wide, deep_local, dn), F32),
            pltpu.VMEM((wide, deep_local, 8 * mid_local), F32),
            pltpu.VMEM((8 * mid_local, chan_deep), BF16),
            pltpu.VMEM((8 * mid_local, chan_deep), BF16),
            pltpu.VMEM((wide, mid_local, cells), F32),
            pltpu.VMEM((wide, mid_local, cells), F32),
            dma((sends,)), dma((wide,)),
            dma((sends,)), dma((wide,)),
            dma((sends,)), dma((wide,)),
            dma, dma,
            dma((nchip,)), dma((nchip,)),
            dma((wide,)), dma((wide,)),
            dma((groups,)), dma((groups,)),
            dma((wide,)), dma((wide,)),
            dma((8,)),
        ],
        compiler_params=pltpu.CompilerParams(
            collective_id=0, has_side_effects=True, vmem_limit_bytes=56 * 1024 * 1024),
    )(
        fine_field,
        w_down_fine.reshape(8 * chan_fine, chan_mid),
        w_conv_mid.reshape(27 * mid_local, chan_mid),
        w_down_mid.reshape(8 * mid_local, chan_deep),
        w_conv_deep.reshape(27 * deep_local, chan_deep),
        w_up_deep,
        w_up_mid.reshape(8 * chan_mid, chan_fine),
        sel,
        fine_sel,
    )


def solution(mesh):
    wide, groups = mesh.shape["wide"], mesh.shape["groups"]
    return jax.shard_map(
        functools.partial(shards, wide, groups),
        mesh=mesh,
        in_specs=(
            P(None, ("groups", "wide"), None),
            P(),
            P(None, "wide", None),
            P(None, "wide", None),
            P(None, "wide", None),
            P(None, "wide", None),
            P(),
        ),
        out_specs=P(None, ("groups", "wide"), None),
        check_vma=False,
    )
```

```python
import functools

import jax
import jax.numpy as jnp
import numpy as np
from jax import lax
from jax.experimental import pallas as pl
from jax.experimental.pallas import tpu as pltpu
from jax.sharding import PartitionSpec as P

YA = 32
ZA = 16
MESH = pl.DeviceIdType.MESH
BF16 = jnp.bfloat16
F32 = jnp.float32


def selector(rows, cols, copies):
    cells = rows * cols
    small = cells // 4
    source = np.arange(copies * cells)[:, None]
    target = np.arange(4 * copies * small)[None, :]
    tap = target // (copies * small)
    copy = target // small % copies
    place = target % small
    row = 2 * (place // (cols // 2)) + tap // 2
    col = 2 * (place % (cols // 2)) + tap % 2
    return (source == copy * cells + row * cols + col).astype(np.float32)


def split(value):
    high = value.astype(BF16)
    return high, (value - high.astype(F32)).astype(BF16)


def dot(left, right):
    return lax.dot_general(left, right, (((1,), (0,)), ((), ())), preferred_element_type=F32)


def dot_nt(left, right):
    return lax.dot_general(left, right, (((1,), (1,)), ((), ())), preferred_element_type=F32)


def dot3(left_high, left_low, right_high, right_low):
    return dot(left_high, right_high) + dot(left_high, right_low) + dot(left_low, right_high)


def middle_kernel(
    wide, groups,
    fine, w_fine_hbm, w_mid_hbm, w_down_hbm, w_deep_hbm, w_up_hbm, w_last_hbm, sel, fsel, out,
    w_fine, w_mid, w_down, w_up_all, w_last, w_up, wfh, wfl, wlh, wll, pacc, xbuf, xh, xl, wmh, wml, acc, mf, wdh, wdl, part, sib, rs, rsin,
    deep_in, wdeep, wch, wcl, deep_out, wup, wuh, wul, mm, landed,
    s1, r1, s2, r2, s3, r3, s_sib, r_sib, s_rs, r_rs, s_up, r_up, s_fw, r_fw, s_aa, r_aa, load_sems,
):
    ny = 2 if wide % 4 == 0 else 1
    nchip = wide // 2
    nz = nchip // ny
    me = lax.axis_index("wide")
    mygroup = lax.axis_index("groups")
    core = me % 2
    chip = me // 2
    y = chip % ny
    z = chip // ny
    mid_local = mf.shape[1]
    chan_mid = xbuf.shape[1]
    cells = mf.shape[2]
    rows, cols = YA // 2, ZA // 2
    drows, dcols = YA // 4, ZA // 4
    dcells = drows * dcols
    deep_local = deep_in.shape[1]
    dn = deep_in.shape[2]
    ngr = dn // cells

    third = wdeep.shape[1]

    def deep_load(k):
        return pltpu.make_async_copy(w_deep_hbm.at[pl.ds(k * third, third)], wdeep.at[k % 2], load_sems.at[5 + k])

    sources = (w_up_hbm, w_fine_hbm, w_mid_hbm, w_down_hbm, w_last_hbm)
    places = (w_up_all, w_fine, w_mid, w_down, w_last)
    loads = [pltpu.make_async_copy(a, b, load_sems.at[k]) for k, (a, b) in enumerate(zip(sources, places))]
    load_up, load_fine, load_mid, load_down, load_last = loads
    for load in loads + [deep_load(0), deep_load(1)]:
        load.start()

    barrier = pltpu.get_barrier_semaphore()
    for step in range(1, wide):
        pl.semaphore_signal(barrier, inc=1, device_id={"wide": (me + step) % wide}, device_id_type=MESH)
    for step in range(1, groups):
        pl.semaphore_signal(barrier, inc=1, device_id={"groups": (mygroup + step) % groups}, device_id_type=MESH)
    pl.semaphore_wait(barrier, wide + groups - 2)

    def slot(zz, yy, cc):
        return (zz * ny + yy) * 2 + cc

    def gather(buf, send_sem, recv_sem, parts, consume, idle):
        piece = buf.shape[1] // parts

        def move(at, target, k, part):
            here = buf.at[at, pl.ds(part * piece, piece)]
            return pltpu.make_async_remote_copy(
                src_ref=here, dst_ref=here, send_sem=send_sem.at[k, part], recv_sem=recv_sem.at[at, part],
                device_id={"wide": target}, device_id_type=MESH)

        def arrived(at, part):
            move(at, slot(z, y, 1 - core), 0, part).wait_recv()

        def all_arrived(at):
            for part in range(parts):
                arrived(at, part)

        sibling = slot(z, y, 1 - core)
        other = slot(z, ny - 1 - y, core)
        for part in range(parts):
            if ny == 2:
                move(me, other, nz, part).start()
            move(me, sibling, 2 * nz, part).start()
        for dz in range(1, nz):
            for part in range(parts):
                move(me, slot((z + nz - dz) % nz, y, core), dz - 1, part).start()
        idle()
        all_arrived(sibling)
        consume(chip)

        def other_row(dz):
            zp = (z + dz) % nz
            at = slot(zp, 1 - y, core)
            for part in range(parts):
                arrived(at, part)
                move(at, sibling, 2 * nz + dz * ny + 1, part).start()

        def step(dz, carry):
            zs = (z + dz) % nz
            at = slot(zs, y, core)
            for part in range(parts):
                arrived(at, part)
                if ny == 2:
                    move(at, other, nz + dz, part).start()
                move(at, sibling, 2 * nz + dz * ny, part).start()
            if ny == 2:
                other_row(dz - 1)
            all_arrived(slot(zs, y, 1 - core))
            consume(zs * ny + y)
            if ny == 2:
                zp = (z + dz - 1) % nz
                all_arrived(slot(zp, 1 - y, 1 - core))
                consume(zp * ny + 1 - y)
            return carry

        lax.fori_loop(1, nz, step, 0)
        if ny == 2:
            other_row(nz - 1)
            zp = (z + nz - 1) % nz
            all_arrived(slot(zp, 1 - y, 1 - core))
            consume(zp * ny + 1 - y)

        def finish():
            keys = list(range(nz - 1)) + list(range(2 * nz, 2 * nz + nz * ny))
            if ny == 2:
                keys += list(range(nz, 2 * nz))
            for k in keys:
                for part in range(parts):
                    move(me, sibling, k, part).wait_send()

        return finish

    share = wup.shape[1] // groups
    mine = pl.ds(pl.multiple_of(mygroup * share, share), share)

    def up_move(target, source):
        return pltpu.make_async_remote_copy(
            src_ref=w_up.at[target], dst_ref=wup.at[me, mine], send_sem=s_up.at[target], recv_sem=r_up.at[source],
            device_id={"wide": target}, device_id_type=MESH)

    def up_arrived(source):
        pltpu.make_async_remote_copy(
            src_ref=w_up.at[source], dst_ref=wup.at[source, mine], send_sem=s_up.at[source], recv_sem=r_up.at[source],
            device_id={"wide": source}, device_id_type=MESH).wait_recv()

    load_up.wait()
    pieces = [w_up_all[t, mine, :] for t in range(8)]
    for d in range(wide):
        w_up[d] = jnp.concatenate([piece[:, d * mid_local:(d + 1) * mid_local] for piece in pieces], axis=1)
    for step in range(1, wide):
        up_move((me + step) % wide, me).start()
    wup[me, mine] = w_up[me]

    chan_fine = fine.shape[0]
    picked_high, picked_low = [], []
    for a in range(2):
        high, low = split(fine[:, a, :])
        high, low = dot_nt(fsel[...], high).astype(BF16), dot_nt(fsel[...], low).astype(BF16)
        for bc in range(4):
            picked_high.append(high[bc * cells:(bc + 1) * cells])
            picked_low.append(low[bc * cells:(bc + 1) * cells])
    picked_high = jnp.concatenate(picked_high, axis=1)
    picked_low = jnp.concatenate(picked_low, axis=1)
    load_fine.wait()

    def split_fine(t, carry):
        here = pl.ds(pl.multiple_of(t * chan_fine, chan_fine), chan_fine)
        wfh[here, :], wfl[here, :] = split(w_fine[here, :])
        return carry

    lax.fori_loop(0, 8, split_fine, 0)
    both = dot(jnp.concatenate([picked_high, picked_low], axis=0), wfh[...])
    xbuf[me] = (both[:cells] + both[cells:] + dot(picked_high, wfl[...])).T
    taps = 9 * mid_local
    lane = lax.broadcasted_iota(jnp.int32, (mid_local, cells), 1)
    mid_masks = {}
    for b in range(3):
        for c in range(3):
            r, s = lane // cols + b - 1, lane % cols + c - 1
            mid_masks[b, c] = (r >= 0) & (r < rows) & (s >= 0) & (s < cols)

    def convolve_mid(at):
        for h in range(2):
            high, low = split(xbuf[at * 2 + h])
            xh[:, h * cells:(h + 1) * cells] = high
            xl[:, h * cells:(h + 1) * cells] = low

        def plane_tap(a, carry):
            here = pl.ds(pl.multiple_of(a * taps, taps), taps)
            product = dot3(wmh[here, :], wml[here, :], xh[...], xl[...])
            for h in range(2):
                total = jnp.zeros((mid_local, cells), F32)
                for b in range(3):
                    for c in range(3):
                        tap = 3 * b + c
                        piece = product[tap * mid_local:(tap + 1) * mid_local, h * cells:(h + 1) * cells]
                        offset = (b - 1) * cols + c - 1
                        if offset:
                            piece = pltpu.roll(piece, (-offset) % cells, 1)
                            piece = jnp.where(mid_masks[b, c], piece, 0.0)
                        total = total + piece
                acc[at * 2 + h - a + 2] += total
            return carry

        lax.fori_loop(0, 3, plane_tap, 0)

    def prepare_mid():
        acc[...] = jnp.zeros_like(acc)
        load_mid.wait()
        load_down.wait()
        wmh[...], wml[...] = split(w_mid[...])
        wdh[...], wdl[...] = split(w_down[...].T)

    finish_mid = gather(xbuf, s1, r1, 2, convolve_mid, prepare_mid)

    mf[...] = jnp.maximum(acc[1:wide + 1], 0.0)

    gathered = []
    for a in range(2):
        for g in range(ngr):
            gathered.append(jnp.concatenate([mf[2 * (4 * g + p) + a] for p in range(4)], axis=1))
    high, low = split(jnp.concatenate(gathered, axis=0))
    high, low = dot(high, sel[...]).astype(BF16), dot(low, sel[...]).astype(BF16)

    def spread_rows(value):
        blocks = []
        for a in range(2):
            for bc in range(4):
                blocks.append(jnp.concatenate([
                    value[(a * ngr + g) * mid_local:(a * ngr + g + 1) * mid_local, bc * cells:(bc + 1) * cells]
                    for g in range(ngr)], axis=1))
        return jnp.concatenate(blocks, axis=0)

    high, low = spread_rows(high), spread_rows(low)
    part[...] = dot3(wdh[...], wdl[...], high, low).reshape(part.shape)
    sibling_id = chip * 2 + 1 - core
    pair = pltpu.make_async_remote_copy(
        src_ref=part.at[:, 1 - core], dst_ref=sib, send_sem=s_sib, recv_sem=r_sib,
        device_id={"wide": sibling_id}, device_id_type=MESH)
    pair.start()

    def split_deep(k):
        def block(t, carry):
            here = pl.ds(pl.multiple_of(t * deep_local, deep_local), deep_local)
            there = pl.ds(pl.multiple_of(k * third + t * deep_local, deep_local), deep_local)
            wch[there, :], wcl[there, :] = split(wdeep[k % 2, here, :])
            return carry

        lax.fori_loop(0, 9, block, 0)

    pair.wait_recv()

    def rs_move(target, source, k):
        return pltpu.make_async_remote_copy(
            src_ref=rs.at[target], dst_ref=rsin.at[source], send_sem=s_rs.at[k], recv_sem=r_rs.at[source],
            device_id={"wide": target * 2 + core}, device_id_type=MESH)

    for step in range(1, nchip):
        target = (chip + step) % nchip
        rs[target] = part[target, core] + sib[target]
        rs_move(target, chip, step).start()
    def forward(target, source):
        return pltpu.make_async_remote_copy(
            src_ref=wup.at[:, mine], dst_ref=wup.at[:, mine], send_sem=s_fw.at[target], recv_sem=r_fw.at[mygroup],
            device_id={"groups": target}, device_id_type=MESH)

    for step in range(1, wide):
        up_arrived((me + wide - step) % wide)
    for step in range(1, groups):
        forward((mygroup + step) % groups, mygroup).start()
    deep_load(0).wait()
    split_deep(0)
    deep_load(2).start()
    deep_load(1).wait()
    split_deep(1)
    deep_load(2).wait()
    split_deep(2)
    load_last.wait()

    def split_last(t, carry):
        here = pl.ds(pl.multiple_of(t * chan_mid, chan_mid), chan_mid)
        wlh[here, :], wll[here, :] = split(w_last[here, :])
        return carry

    lax.fori_loop(0, 8, split_last, 0)
    total = part[chip, core] + sib[chip]
    for step in range(1, nchip):
        source = (chip + nchip - step) % nchip
        rs_move(source, source, step).wait_recv()
        total = total + rsin[source]
    deep_in[me] = jnp.maximum(total, 0.0)

    def nothing(*args):
        return None

    def prepare_deep():
        for step in range(1, groups):
            source = (mygroup + groups - step) % groups
            theirs = pl.ds(pl.multiple_of(source * share, share), share)
            pltpu.make_async_remote_copy(
                src_ref=wup.at[:, theirs], dst_ref=wup.at[:, theirs], send_sem=s_fw.at[source],
                recv_sem=r_fw.at[source], device_id={"groups": source}, device_id_type=MESH).wait_recv()
        wuh[...], wul[...] = split(wup[...].reshape(wide * deep_local, wup.shape[2]).T)

    chip_rows = 2 * deep_local
    by_chip = chip_rows % 128 == 0

    def convolve_deep(at):
        high, low = split(deep_in[pl.ds(at * 2, 2)].reshape(chip_rows, dn))
        lanes = pl.ds(pl.multiple_of(at * chip_rows, chip_rows), chip_rows)

        def plane_tap(a, carry):
            here = pl.ds(pl.multiple_of(a * 9 * deep_local, 9 * deep_local), 9 * deep_local)
            pacc[here, :] += dot3(wch[here, lanes], wcl[here, lanes], high, low)
            return carry

        lax.fori_loop(0, 3, plane_tap, 0)

    if by_chip:
        pacc[...] = jnp.zeros_like(pacc)
        finish_in = gather(deep_in, s2, r2, 1, convolve_deep, prepare_deep)
    else:
        finish_in = gather(deep_in, s2, r2, 1, nothing, prepare_deep)
        dh, dl = split(deep_in[...].reshape(wide * deep_local, dn))
        pacc[...] = dot3(wch[...], wcl[...], dh, dl)
    dlane = lax.broadcasted_iota(jnp.int32, (deep_local, dn), 1)
    total = jnp.zeros((deep_local, dn), F32)
    for a in range(3):
        for b in range(3):
            for c in range(3):
                tap = 3 * b + c
                at = (9 * a + tap) * deep_local
                piece = pacc[at:at + deep_local, :]
                offset = (a - 1) * dcells + (b - 1) * dcols + c - 1
                if offset:
                    piece = pltpu.roll(piece, (-offset) % dn, 1)
                    p, r, s = dlane // dcells + a - 1, dlane // dcols % drows + b - 1, dlane % dcols + c - 1
                    inside = (p >= 0) & (p < dn // dcells) & (r >= 0) & (r < drows) & (s >= 0) & (s < dcols)
                    piece = jnp.where(inside, piece, 0.0)
                total = total + piece
    deep_out[me] = jnp.maximum(total, 0.0)

    finish_out = gather(deep_out, s3, r3, 1, nothing, nothing)
    dh, dl = split(deep_out[...].reshape(wide * deep_local, dn))
    lifted = dot3(wuh[...], wul[...], dh, dl)
    blocks = []
    for a in range(2):
        for g in range(ngr):
            blocks.append(jnp.concatenate([
                lifted[(a * 4 + bc) * mid_local:(a * 4 + bc + 1) * mid_local, g * cells:(g + 1) * cells]
                for bc in range(4)], axis=1))
    high, low = split(jnp.concatenate(blocks, axis=0))
    spread = dot_nt(high, sel[...]) + dot_nt(low, sel[...])
    for a in range(2):
        for g in range(ngr):
            for p in range(4):
                plane = 2 * (4 * g + p) + a
                block = spread[(a * ngr + g) * mid_local:(a * ngr + g + 1) * mid_local, p * cells:(p + 1) * cells]
                mm[plane] = jnp.maximum(mf[plane] + block, 0.0)

    def plane_move(target, source):
        return pltpu.make_async_remote_copy(
            src_ref=mm.at[target], dst_ref=landed.at[source], send_sem=s_aa.at[target], recv_sem=r_aa.at[source],
            device_id={"wide": target}, device_id_type=MESH)

    for step in range(1, wide):
        plane_move((me + step) % wide, me).start()
    landed[me] = mm[me]
    finish_mid()
    finish_in()
    finish_out()
    pair.wait_send()
    for step in range(1, nchip):
        rs_move((chip + step) % nchip, chip, step).wait_send()
    for step in range(1, wide):
        up_move((me + step) % wide, me).wait_send()
    for step in range(1, groups):
        forward((mygroup + step) % groups, mygroup).wait_send()
    for step in range(1, wide):
        plane_move((me + step) % wide, me).wait_send()
    for step in range(1, wide):
        source = (me + wide - step) % wide
        plane_move(source, source).wait_recv()

    high, low = split(landed[...].reshape(chan_mid, cells).T)
    both = jnp.concatenate([high, low], axis=0)
    for a in range(2):
        rows_of = []
        for bc in range(4):
            here = pl.ds((4 * a + bc) * chan_mid, chan_mid)
            twice = dot(both, wlh[here, :])
            rows_of.append(twice[:cells] + twice[cells:] + dot(high, wll[here, :]))
        last_high, last_low = split(jnp.concatenate(rows_of, axis=0).T)
        out[a] = dot(last_high, fsel[...]) + dot(last_low, fsel[...])


def shards(wide, groups, fine_field, w_down_fine, w_conv_mid, w_down_mid, w_conv_deep, w_up_deep, w_up_mid):
    chan_fine = fine_field.shape[0]
    chan_mid = w_down_fine.shape[2]
    chan_deep = w_down_mid.shape[2]
    mid_local = w_conv_mid.shape[1]
    deep_local = w_conv_deep.shape[1]
    cells = YA // 2 * (ZA // 2)
    dn = wide // 2 * (cells // 4)
    nchip = wide // 2
    fine_sel = jnp.asarray(selector(YA, ZA, 1).T, dtype=BF16)
    sel = jnp.asarray(selector(YA // 2, ZA // 2, 4), dtype=BF16)

    vmem = pl.BlockSpec(memory_space=pltpu.VMEM)
    dma = pltpu.SemaphoreType.DMA
    sends = 4 * nchip
    anywhere = pl.BlockSpec(memory_space=pl.ANY)
    turned = pl.pallas_call(
        functools.partial(middle_kernel, wide, groups),
        out_shape=jax.ShapeDtypeStruct((2, chan_fine, YA * ZA), F32),
        in_specs=[vmem] + [anywhere] * 6 + [vmem, vmem],
        out_specs=vmem,
        scratch_shapes=[
            pltpu.VMEM((8 * chan_fine, chan_mid), F32),
            pltpu.VMEM((27 * mid_local, chan_mid), F32),
            pltpu.VMEM((8 * mid_local, chan_deep), F32),
            pltpu.VMEM((8, deep_local, chan_mid), F32),
            pltpu.VMEM((8 * chan_mid, chan_fine), F32),
            pltpu.VMEM((wide, deep_local // groups, 8 * mid_local), F32),
            pltpu.VMEM((8 * chan_fine, chan_mid), BF16),
            pltpu.VMEM((8 * chan_fine, chan_mid), BF16),
            pltpu.VMEM((8 * chan_mid, chan_fine), BF16),
            pltpu.VMEM((8 * chan_mid, chan_fine), BF16),
            pltpu.VMEM((27 * deep_local, dn), F32),
            pltpu.VMEM((wide, chan_mid, cells), F32),
            pltpu.VMEM((chan_mid, 2 * cells), BF16),
            pltpu.VMEM((chan_mid, 2 * cells), BF16),
            pltpu.VMEM((27 * mid_local, chan_mid), BF16),
            pltpu.VMEM((27 * mid_local, chan_mid), BF16),
            pltpu.VMEM((wide + 2, mid_local, cells), F32),
            pltpu.VMEM((wide, mid_local, cells), F32),
            pltpu.VMEM((chan_deep, 8 * mid_local), BF16),
            pltpu.VMEM((chan_deep, 8 * mid_local), BF16),
            pltpu.VMEM((nchip, 2, deep_local, dn), F32),
            pltpu.VMEM((nchip, deep_local, dn), F32),
            pltpu.VMEM((nchip, deep_local, dn), F32),
            pltpu.VMEM((nchip, deep_local, dn), F32),
            pltpu.VMEM((wide, deep_local, dn), F32),
            pltpu.VMEM((2, 9 * deep_local, chan_deep), F32),
            pltpu.VMEM((27 * deep_local, chan_deep), BF16),
            pltpu.VMEM((27 * deep_local, chan_deep), BF16),
            pltpu.VMEM((wide, deep_local, dn), F32),
            pltpu.VMEM((wide, deep_local, 8 * mid_local), F32),
            pltpu.VMEM((8 * mid_local, chan_deep), BF16),
            pltpu.VMEM((8 * mid_local, chan_deep), BF16),
            pltpu.VMEM((wide, mid_local, cells), F32),
            pltpu.VMEM((wide, mid_local, cells), F32),
            dma((sends, 2)), dma((wide, 2)),
            dma((sends, 1)), dma((wide, 1)),
            dma((sends, 1)), dma((wide, 1)),
            dma, dma,
            dma((nchip,)), dma((nchip,)),
            dma((wide,)), dma((wide,)),
            dma((groups,)), dma((groups,)),
            dma((wide,)), dma((wide,)),
            dma((8,)),
        ],
        compiler_params=pltpu.CompilerParams(
            collective_id=0, has_side_effects=True, vmem_limit_bytes=56 * 1024 * 1024),
    )(
        fine_field,
        w_down_fine.reshape(8 * chan_fine, chan_mid),
        w_conv_mid.reshape(27 * mid_local, chan_mid),
        w_down_mid.reshape(8 * mid_local, chan_deep),
        w_conv_deep.reshape(27 * deep_local, chan_deep),
        w_up_deep,
        w_up_mid.reshape(8 * chan_mid, chan_fine),
        sel,
        fine_sel,
    )
    return turned.transpose(1, 0, 2)


def solution(mesh):
    wide, groups = mesh.shape["wide"], mesh.shape["groups"]
    return jax.shard_map(
        functools.partial(shards, wide, groups),
        mesh=mesh,
        in_specs=(
            P(None, ("groups", "wide"), None),
            P(),
            P(None, "wide", None),
            P(None, "wide", None),
            P(None, "wide", None),
            P(None, "wide", None),
            P(),
        ),
        out_specs=P(None, ("groups", "wide"), None),
        check_vma=False,
    )
```

```python
import functools

import jax
import jax.numpy as jnp
import numpy as np
from jax import lax
from jax.experimental import pallas as pl
from jax.experimental.pallas import tpu as pltpu
from jax.sharding import PartitionSpec as P

YA = 32
ZA = 16
MESH = pl.DeviceIdType.MESH
BF16 = jnp.bfloat16
F32 = jnp.float32


def selector(rows, cols, copies):
    cells = rows * cols
    small = cells // 4
    source = np.arange(copies * cells)[:, None]
    target = np.arange(4 * copies * small)[None, :]
    tap = target // (copies * small)
    copy = target // small % copies
    place = target % small
    row = 2 * (place // (cols // 2)) + tap // 2
    col = 2 * (place % (cols // 2)) + tap % 2
    return (source == copy * cells + row * cols + col).astype(np.float32)


def split(value):
    high = value.astype(BF16)
    return high, (value - high.astype(F32)).astype(BF16)


def dot(left, right):
    return lax.dot_general(left, right, (((1,), (0,)), ((), ())), preferred_element_type=F32)


def dot_nt(left, right):
    return lax.dot_general(left, right, (((1,), (1,)), ((), ())), preferred_element_type=F32)


def dot3(left_high, left_low, right_high, right_low):
    return dot(left_high, right_high) + dot(left_high, right_low) + dot(left_low, right_high)


def middle_kernel(
    wide, groups,
    fine, w_fine_hbm, w_mid_hbm, w_down_hbm, w_deep_hbm, w_up_hbm, w_last_hbm, sel, fsel, out,
    w_fine, w_mid, w_down, w_up_all, w_last, w_up, wfh, wfl, wlh, wll, pacc, xbuf, xh, xl, wmh, wml, acc, mf, wdh, wdl, part, sib, rs, rsin,
    deep_in, wdeep, wch, wcl, deep_out, wup, wuh, wul, mm, landed,
    s1, r1, s2, r2, s3, r3, s_sib, r_sib, s_rs, r_rs, s_up, r_up, s_fw, r_fw, s_aa, r_aa, load_sems,
):
    ny = 2 if wide % 4 == 0 else 1
    nchip = wide // 2
    nz = nchip // ny
    me = lax.axis_index("wide")
    mygroup = lax.axis_index("groups")
    core = me % 2
    chip = me // 2
    y = chip % ny
    z = chip // ny
    mid_local = mf.shape[1]
    chan_mid = xbuf.shape[1]
    cells = mf.shape[2]
    rows, cols = YA // 2, ZA // 2
    drows, dcols = YA // 4, ZA // 4
    dcells = drows * dcols
    deep_local = deep_in.shape[1]
    dn = deep_in.shape[2]
    ngr = dn // cells

    third = wdeep.shape[1]

    def deep_load(k):
        return pltpu.make_async_copy(w_deep_hbm.at[pl.ds(k * third, third)], wdeep.at[k % 2], load_sems.at[5 + k])

    sources = (w_up_hbm, w_fine_hbm, w_mid_hbm, w_down_hbm, w_last_hbm)
    places = (w_up_all, w_fine, w_mid, w_down, w_last)
    loads = [pltpu.make_async_copy(a, b, load_sems.at[k]) for k, (a, b) in enumerate(zip(sources, places))]
    load_up, load_fine, load_mid, load_down, load_last = loads
    for load in loads + [deep_load(0), deep_load(1)]:
        load.start()

    barrier = pltpu.get_barrier_semaphore()
    for step in range(1, wide):
        pl.semaphore_signal(barrier, inc=1, device_id={"wide": (me + step) % wide}, device_id_type=MESH)
    for step in range(1, groups):
        pl.semaphore_signal(barrier, inc=1, device_id={"groups": (mygroup + step) % groups}, device_id_type=MESH)
    pl.semaphore_wait(barrier, wide + groups - 2)

    def slot(zz, yy, cc):
        return (zz * ny + yy) * 2 + cc

    def gather(buf, send_sem, recv_sem, parts, consume, idle):
        piece = buf.shape[1] // parts

        def move(at, target, k, part):
            here = buf.at[at, pl.ds(part * piece, piece)]
            return pltpu.make_async_remote_copy(
                src_ref=here, dst_ref=here, send_sem=send_sem.at[k, part], recv_sem=recv_sem.at[at, part],
                device_id={"wide": target}, device_id_type=MESH)

        def arrived(at, part):
            move(at, slot(z, y, 1 - core), 0, part).wait_recv()

        def all_arrived(at):
            for part in range(parts):
                arrived(at, part)

        sibling = slot(z, y, 1 - core)
        other = slot(z, ny - 1 - y, core)
        for part in range(parts):
            if ny == 2:
                move(me, other, nz, part).start()
            move(me, sibling, 2 * nz, part).start()
        for dz in range(1, nz):
            for part in range(parts):
                move(me, slot((z + nz - dz) % nz, y, core), dz - 1, part).start()
        idle()
        all_arrived(sibling)
        consume(chip)

        def other_row(dz):
            zp = (z + dz) % nz
            at = slot(zp, 1 - y, core)
            for part in range(parts):
                arrived(at, part)
                move(at, sibling, 2 * nz + dz * ny + 1, part).start()

        def step(dz, carry):
            zs = (z + dz) % nz
            at = slot(zs, y, core)
            for part in range(parts):
                arrived(at, part)
                if ny == 2:
                    move(at, other, nz + dz, part).start()
                move(at, sibling, 2 * nz + dz * ny, part).start()
            if ny == 2:
                other_row(dz - 1)
            all_arrived(slot(zs, y, 1 - core))
            consume(zs * ny + y)
            if ny == 2:
                zp = (z + dz - 1) % nz
                all_arrived(slot(zp, 1 - y, 1 - core))
                consume(zp * ny + 1 - y)
            return carry

        lax.fori_loop(1, nz, step, 0)
        if ny == 2:
            other_row(nz - 1)
            zp = (z + nz - 1) % nz
            all_arrived(slot(zp, 1 - y, 1 - core))
            consume(zp * ny + 1 - y)

        def finish():
            keys = list(range(nz - 1)) + list(range(2 * nz, 2 * nz + nz * ny))
            if ny == 2:
                keys += list(range(nz, 2 * nz))
            for k in keys:
                for part in range(parts):
                    move(me, sibling, k, part).wait_send()

        return finish

    share = wup.shape[1] // groups
    mine = pl.ds(pl.multiple_of(mygroup * share, share), share)

    def up_move(target, source):
        return pltpu.make_async_remote_copy(
            src_ref=w_up.at[target], dst_ref=wup.at[me, mine], send_sem=s_up.at[target], recv_sem=r_up.at[source],
            device_id={"wide": target}, device_id_type=MESH)

    def up_arrived(source):
        pltpu.make_async_remote_copy(
            src_ref=w_up.at[source], dst_ref=wup.at[source, mine], send_sem=s_up.at[source], recv_sem=r_up.at[source],
            device_id={"wide": source}, device_id_type=MESH).wait_recv()

    load_up.wait()
    pieces = [w_up_all[t, mine, :] for t in range(8)]
    for d in range(wide):
        w_up[d] = jnp.concatenate([piece[:, d * mid_local:(d + 1) * mid_local] for piece in pieces], axis=1)
    wup[me, mine] = w_up[me]

    chan_fine = fine.shape[0]
    picked_high, picked_low = [], []
    for a in range(2):
        high, low = split(fine[:, a, :])
        high, low = dot_nt(fsel[...], high).astype(BF16), dot_nt(fsel[...], low).astype(BF16)
        for bc in range(4):
            picked_high.append(high[bc * cells:(bc + 1) * cells])
            picked_low.append(low[bc * cells:(bc + 1) * cells])
    picked_high = jnp.concatenate(picked_high, axis=1)
    picked_low = jnp.concatenate(picked_low, axis=1)
    load_fine.wait()

    def split_fine(t, carry):
        here = pl.ds(pl.multiple_of(t * chan_fine, chan_fine), chan_fine)
        wfh[here, :], wfl[here, :] = split(w_fine[here, :])
        return carry

    lax.fori_loop(0, 8, split_fine, 0)
    both = dot(jnp.concatenate([picked_high, picked_low], axis=0), wfh[...])
    xbuf[me] = (both[:cells] + both[cells:] + dot(picked_high, wfl[...])).T
    taps = 9 * mid_local
    lane = lax.broadcasted_iota(jnp.int32, (mid_local, cells), 1)
    mid_masks = {}
    for b in range(3):
        for c in range(3):
            r, s = lane // cols + b - 1, lane % cols + c - 1
            mid_masks[b, c] = (r >= 0) & (r < rows) & (s >= 0) & (s < cols)

    def convolve_mid(at):
        for h in range(2):
            high, low = split(xbuf[at * 2 + h])
            xh[:, h * cells:(h + 1) * cells] = high
            xl[:, h * cells:(h + 1) * cells] = low

        def plane_tap(a, carry):
            here = pl.ds(pl.multiple_of(a * taps, taps), taps)
            product = dot3(wmh[here, :], wml[here, :], xh[...], xl[...])
            for h in range(2):
                total = jnp.zeros((mid_local, cells), F32)
                for b in range(3):
                    for c in range(3):
                        tap = 3 * b + c
                        piece = product[tap * mid_local:(tap + 1) * mid_local, h * cells:(h + 1) * cells]
                        offset = (b - 1) * cols + c - 1
                        if offset:
                            piece = pltpu.roll(piece, (-offset) % cells, 1)
                            piece = jnp.where(mid_masks[b, c], piece, 0.0)
                        total = total + piece
                acc[at * 2 + h - a + 2] += total
            return carry

        lax.fori_loop(0, 3, plane_tap, 0)

    def prepare_mid():
        acc[...] = jnp.zeros_like(acc)
        load_mid.wait()
        load_down.wait()
        wmh[...], wml[...] = split(w_mid[...])
        wdh[...], wdl[...] = split(w_down[...].T)

    finish_mid = gather(xbuf, s1, r1, 2, convolve_mid, prepare_mid)

    for step in range(1, wide):
        up_move((me + step) % wide, me).start()
    mf[...] = jnp.maximum(acc[1:wide + 1], 0.0)

    gathered = []
    for a in range(2):
        for g in range(ngr):
            gathered.append(jnp.concatenate([mf[2 * (4 * g + p) + a] for p in range(4)], axis=1))
    high, low = split(jnp.concatenate(gathered, axis=0))
    high, low = dot(high, sel[...]).astype(BF16), dot(low, sel[...]).astype(BF16)

    def spread_rows(value):
        blocks = []
        for a in range(2):
            for bc in range(4):
                blocks.append(jnp.concatenate([
                    value[(a * ngr + g) * mid_local:(a * ngr + g + 1) * mid_local, bc * cells:(bc + 1) * cells]
                    for g in range(ngr)], axis=1))
        return jnp.concatenate(blocks, axis=0)

    high, low = spread_rows(high), spread_rows(low)
    part[...] = dot3(wdh[...], wdl[...], high, low).reshape(part.shape)
    sibling_id = chip * 2 + 1 - core
    pair = pltpu.make_async_remote_copy(
        src_ref=part.at[:, 1 - core], dst_ref=sib, send_sem=s_sib, recv_sem=r_sib,
        device_id={"wide": sibling_id}, device_id_type=MESH)
    pair.start()

    def split_deep(k):
        def block(t, carry):
            here = pl.ds(pl.multiple_of(t * deep_local, deep_local), deep_local)
            there = pl.ds(pl.multiple_of(k * third + t * deep_local, deep_local), deep_local)
            wch[there, :], wcl[there, :] = split(wdeep[k % 2, here, :])
            return carry

        lax.fori_loop(0, 9, block, 0)

    pair.wait_recv()

    def rs_move(target, source, k):
        return pltpu.make_async_remote_copy(
            src_ref=rs.at[target], dst_ref=rsin.at[source], send_sem=s_rs.at[k], recv_sem=r_rs.at[source],
            device_id={"wide": target * 2 + core}, device_id_type=MESH)

    for step in range(1, nchip):
        target = (chip + step) % nchip
        rs[target] = part[target, core] + sib[target]
        rs_move(target, chip, step).start()
    def forward(target, source):
        return pltpu.make_async_remote_copy(
            src_ref=wup.at[:, mine], dst_ref=wup.at[:, mine], send_sem=s_fw.at[target], recv_sem=r_fw.at[mygroup],
            device_id={"groups": target}, device_id_type=MESH)

    deep_load(0).wait()
    split_deep(0)
    deep_load(2).start()
    deep_load(1).wait()
    split_deep(1)
    deep_load(2).wait()
    split_deep(2)
    load_last.wait()

    def split_last(t, carry):
        here = pl.ds(pl.multiple_of(t * chan_mid, chan_mid), chan_mid)
        wlh[here, :], wll[here, :] = split(w_last[here, :])
        return carry

    lax.fori_loop(0, 8, split_last, 0)
    total = part[chip, core] + sib[chip]
    for step in range(1, nchip):
        source = (chip + nchip - step) % nchip
        rs_move(source, source, step).wait_recv()
        total = total + rsin[source]
    deep_in[me] = jnp.maximum(total, 0.0)

    def nothing(*args):
        return None

    def prepare_deep():
        for step in range(1, wide):
            up_arrived((me + wide - step) % wide)
        for step in range(1, groups):
            forward((mygroup + step) % groups, mygroup).start()

    chip_rows = 2 * deep_local
    by_chip = chip_rows % 128 == 0

    def convolve_deep(at):
        high, low = split(deep_in[pl.ds(at * 2, 2)].reshape(chip_rows, dn))
        lanes = pl.ds(pl.multiple_of(at * chip_rows, chip_rows), chip_rows)

        def plane_tap(a, carry):
            here = pl.ds(pl.multiple_of(a * 9 * deep_local, 9 * deep_local), 9 * deep_local)
            pacc[here, :] += dot3(wch[here, lanes], wcl[here, lanes], high, low)
            return carry

        lax.fori_loop(0, 3, plane_tap, 0)

    if by_chip:
        pacc[...] = jnp.zeros_like(pacc)
        finish_in = gather(deep_in, s2, r2, 1, convolve_deep, prepare_deep)
    else:
        finish_in = gather(deep_in, s2, r2, 1, nothing, prepare_deep)
        dh, dl = split(deep_in[...].reshape(wide * deep_local, dn))
        pacc[...] = dot3(wch[...], wcl[...], dh, dl)
    dlane = lax.broadcasted_iota(jnp.int32, (deep_local, dn), 1)
    total = jnp.zeros((deep_local, dn), F32)
    for a in range(3):
        for b in range(3):
            for c in range(3):
                tap = 3 * b + c
                at = (9 * a + tap) * deep_local
                piece = pacc[at:at + deep_local, :]
                offset = (a - 1) * dcells + (b - 1) * dcols + c - 1
                if offset:
                    piece = pltpu.roll(piece, (-offset) % dn, 1)
                    p, r, s = dlane // dcells + a - 1, dlane // dcols % drows + b - 1, dlane % dcols + c - 1
                    inside = (p >= 0) & (p < dn // dcells) & (r >= 0) & (r < drows) & (s >= 0) & (s < dcols)
                    piece = jnp.where(inside, piece, 0.0)
                total = total + piece
    deep_out[me] = jnp.maximum(total, 0.0)

    def prepare_up():
        for step in range(1, groups):
            source = (mygroup + groups - step) % groups
            theirs = pl.ds(pl.multiple_of(source * share, share), share)
            pltpu.make_async_remote_copy(
                src_ref=wup.at[:, theirs], dst_ref=wup.at[:, theirs], send_sem=s_fw.at[source],
                recv_sem=r_fw.at[source], device_id={"groups": source}, device_id_type=MESH).wait_recv()
        wuh[...], wul[...] = split(wup[...].reshape(wide * deep_local, wup.shape[2]).T)

    finish_out = gather(deep_out, s3, r3, 1, nothing, prepare_up)
    dh, dl = split(deep_out[...].reshape(wide * deep_local, dn))
    lifted = dot3(wuh[...], wul[...], dh, dl)
    blocks = []
    for a in range(2):
        for g in range(ngr):
            blocks.append(jnp.concatenate([
                lifted[(a * 4 + bc) * mid_local:(a * 4 + bc + 1) * mid_local, g * cells:(g + 1) * cells]
                for bc in range(4)], axis=1))
    high, low = split(jnp.concatenate(blocks, axis=0))
    spread = dot_nt(high, sel[...]) + dot_nt(low, sel[...])
    for a in range(2):
        for g in range(ngr):
            for p in range(4):
                plane = 2 * (4 * g + p) + a
                block = spread[(a * ngr + g) * mid_local:(a * ngr + g + 1) * mid_local, p * cells:(p + 1) * cells]
                mm[plane] = jnp.maximum(mf[plane] + block, 0.0)

    def plane_move(target, source):
        return pltpu.make_async_remote_copy(
            src_ref=mm.at[target], dst_ref=landed.at[source], send_sem=s_aa.at[target], recv_sem=r_aa.at[source],
            device_id={"wide": target}, device_id_type=MESH)

    for step in range(1, wide):
        plane_move((me + step) % wide, me).start()
    landed[me] = mm[me]
    finish_mid()
    finish_in()
    finish_out()
    pair.wait_send()
    for step in range(1, nchip):
        rs_move((chip + step) % nchip, chip, step).wait_send()
    for step in range(1, wide):
        up_move((me + step) % wide, me).wait_send()
    for step in range(1, groups):
        forward((mygroup + step) % groups, mygroup).wait_send()
    for step in range(1, wide):
        plane_move((me + step) % wide, me).wait_send()
    for step in range(1, wide):
        source = (me + wide - step) % wide
        plane_move(source, source).wait_recv()

    high, low = split(landed[...].reshape(chan_mid, cells).T)
    both = jnp.concatenate([high, low], axis=0)
    for a in range(2):
        rows_of = []
        for bc in range(4):
            here = pl.ds((4 * a + bc) * chan_mid, chan_mid)
            twice = dot(both, wlh[here, :])
            rows_of.append(twice[:cells] + twice[cells:] + dot(high, wll[here, :]))
        last_high, last_low = split(jnp.concatenate(rows_of, axis=0).T)
        out[a] = dot(last_high, fsel[...]) + dot(last_low, fsel[...])


def shards(wide, groups, fine_field, w_down_fine, w_conv_mid, w_down_mid, w_conv_deep, w_up_deep, w_up_mid):
    chan_fine = fine_field.shape[0]
    chan_mid = w_down_fine.shape[2]
    chan_deep = w_down_mid.shape[2]
    mid_local = w_conv_mid.shape[1]
    deep_local = w_conv_deep.shape[1]
    cells = YA // 2 * (ZA // 2)
    dn = wide // 2 * (cells // 4)
    nchip = wide // 2
    fine_sel = jnp.asarray(selector(YA, ZA, 1).T, dtype=BF16)
    sel = jnp.asarray(selector(YA // 2, ZA // 2, 4), dtype=BF16)

    vmem = pl.BlockSpec(memory_space=pltpu.VMEM)
    dma = pltpu.SemaphoreType.DMA
    sends = 4 * nchip
    anywhere = pl.BlockSpec(memory_space=pl.ANY)
    turned = pl.pallas_call(
        functools.partial(middle_kernel, wide, groups),
        out_shape=jax.ShapeDtypeStruct((2, chan_fine, YA * ZA), F32),
        in_specs=[vmem] + [anywhere] * 6 + [vmem, vmem],
        out_specs=vmem,
        scratch_shapes=[
            pltpu.VMEM((8 * chan_fine, chan_mid), F32),
            pltpu.VMEM((27 * mid_local, chan_mid), F32),
            pltpu.VMEM((8 * mid_local, chan_deep), F32),
            pltpu.VMEM((8, deep_local, chan_mid), F32),
            pltpu.VMEM((8 * chan_mid, chan_fine), F32),
            pltpu.VMEM((wide, deep_local // groups, 8 * mid_local), F32),
            pltpu.VMEM((8 * chan_fine, chan_mid), BF16),
            pltpu.VMEM((8 * chan_fine, chan_mid), BF16),
            pltpu.VMEM((8 * chan_mid, chan_fine), BF16),
            pltpu.VMEM((8 * chan_mid, chan_fine), BF16),
            pltpu.VMEM((27 * deep_local, dn), F32),
            pltpu.VMEM((wide, chan_mid, cells), F32),
            pltpu.VMEM((chan_mid, 2 * cells), BF16),
            pltpu.VMEM((chan_mid, 2 * cells), BF16),
            pltpu.VMEM((27 * mid_local, chan_mid), BF16),
            pltpu.VMEM((27 * mid_local, chan_mid), BF16),
            pltpu.VMEM((wide + 2, mid_local, cells), F32),
            pltpu.VMEM((wide, mid_local, cells), F32),
            pltpu.VMEM((chan_deep, 8 * mid_local), BF16),
            pltpu.VMEM((chan_deep, 8 * mid_local), BF16),
            pltpu.VMEM((nchip, 2, deep_local, dn), F32),
            pltpu.VMEM((nchip, deep_local, dn), F32),
            pltpu.VMEM((nchip, deep_local, dn), F32),
            pltpu.VMEM((nchip, deep_local, dn), F32),
            pltpu.VMEM((wide, deep_local, dn), F32),
            pltpu.VMEM((2, 9 * deep_local, chan_deep), F32),
            pltpu.VMEM((27 * deep_local, chan_deep), BF16),
            pltpu.VMEM((27 * deep_local, chan_deep), BF16),
            pltpu.VMEM((wide, deep_local, dn), F32),
            pltpu.VMEM((wide, deep_local, 8 * mid_local), F32),
            pltpu.VMEM((8 * mid_local, chan_deep), BF16),
            pltpu.VMEM((8 * mid_local, chan_deep), BF16),
            pltpu.VMEM((wide, mid_local, cells), F32),
            pltpu.VMEM((wide, mid_local, cells), F32),
            dma((sends, 2)), dma((wide, 2)),
            dma((sends, 1)), dma((wide, 1)),
            dma((sends, 1)), dma((wide, 1)),
            dma, dma,
            dma((nchip,)), dma((nchip,)),
            dma((wide,)), dma((wide,)),
            dma((groups,)), dma((groups,)),
            dma((wide,)), dma((wide,)),
            dma((8,)),
        ],
        compiler_params=pltpu.CompilerParams(
            collective_id=0, has_side_effects=True, vmem_limit_bytes=56 * 1024 * 1024),
    )(
        fine_field,
        w_down_fine.reshape(8 * chan_fine, chan_mid),
        w_conv_mid.reshape(27 * mid_local, chan_mid),
        w_down_mid.reshape(8 * mid_local, chan_deep),
        w_conv_deep.reshape(27 * deep_local, chan_deep),
        w_up_deep,
        w_up_mid.reshape(8 * chan_mid, chan_fine),
        sel,
        fine_sel,
    )
    return turned.transpose(1, 0, 2)


def solution(mesh):
    wide, groups = mesh.shape["wide"], mesh.shape["groups"]
    return jax.shard_map(
        functools.partial(shards, wide, groups),
        mesh=mesh,
        in_specs=(
            P(None, ("groups", "wide"), None),
            P(),
            P(None, "wide", None),
            P(None, "wide", None),
            P(None, "wide", None),
            P(None, "wide", None),
            P(),
        ),
        out_specs=P(None, ("groups", "wide"), None),
        check_vma=False,
    )
```
